512 devices in a mesh: dp: 32 (over y, x), fsdp: 16 (over z, core).
Axes of the slice: x: 4, y: 8, z: 8, core: 2. Of those that a mesh axis runs over, the one named last changes fastest.
Arguments:
- layer_input: bfloat16 [65536, 8192], P(('dp', 'fsdp')), may hold values from -24 to 24
- norm_gain: float32 [8192], P('fsdp'), may hold values from 0.4 to 2.4
- value_weight: bfloat16 [8192, 512], P('fsdp'), may hold values from -0.25 to 0.25
- value_cotangent: bfloat16 [65536, 512], P(('dp', 'fsdp')), may hold values from -36 to 36
Outputs:
- input_grad: bfloat16 [65536, 8192], P(('dp', 'fsdp'))
- weight_update: bfloat16 [8192, 512], P('fsdp', 'dp')
- gain_update: bfloat16 [8192], P('fsdp')
The draws below stay inside these ranges and needn't reach their ends.
All inputs are finite; a program needn't handle non-finite values.
Results may differ from the reference program's by a relative error of at most 0.015.
Values may be sent and summed in bfloat16 or wider, within the bound.
No kernel may reach another device: no remote copies, remote signals or barrier semaphores. Data moves between devices by JAX's collectives and lax.ppermute only.
A program may use at most 64 MiB of HBM per device.

```python
import math
import jax
import jax.numpy as jnp
import numpy as np
from jax import lax

D = 8192
W = 512
REPL_TOK = 2048
TOKENS = 65536
LEVELS = 5
N_DP = 32


def shared_mix(key, width, low_end, high_end, rep_low, rep_high):
    count_repl = TOKENS // REPL_TOK
    factor = jax.random.uniform(jax.random.fold_in(key, 77), (count_repl,), jnp.float32, rep_low, rep_high)
    flipped = jax.random.bernoulli(jax.random.fold_in(key, 91 + width), 0.5, ())
    position = (jnp.arange(width).astype(jnp.float32) + 0.5) / width
    position = jnp.where(flipped, 1.0 - position, position)
    ramp = low_end + (high_end - low_end) * position
    return factor[:, None] * ramp[None, :]


def blended(key, width, low_end, high_end, rep_low, rep_high, scale_low, scale_high):
    mixing = shared_mix(key, width, low_end, high_end, rep_low, rep_high)
    key = jax.random.fold_in(key, width + 5)
    key_common, key_own, key_rows = jax.random.split(key, 3)
    common = jnp.clip(jax.random.normal(key_common, (REPL_TOK, width), jnp.float32), -4.0, 4.0)
    own = jnp.clip(jax.random.normal(key_own, (TOKENS, width), jnp.float32), -4.0, 4.0)
    replica = jnp.arange(TOKENS) // REPL_TOK
    weight_shared = mixing[replica]
    tiled = jnp.tile(common, (TOKENS // REPL_TOK, 1))
    row_scales = jnp.exp(jax.random.uniform(key_rows, (TOKENS, 1), jnp.float32, jnp.log(scale_low), jnp.log(scale_high)))
    return (row_scales * (weight_shared * tiled + jnp.sqrt(1.0 - weight_shared * weight_shared) * own), replica)


def draw_layer_input(key, part):
    low_end, high_end, rep_low, rep_high = (0.05, 0.95, 0.5, 1.0)
    values, replica = blended(key, D, low_end, high_end, rep_low, rep_high, 0.5, 4.0)
    return values.astype(jnp.bfloat16)


def draw_value_cotangent(key, part):
    low_end, high_end, rep_low, rep_high = (0.05, 0.95, 0.5, 1.0)
    values, replica = blended(key, W, low_end, high_end, rep_low, rep_high, 0.5, 2.0)
    count_repl = TOKENS // REPL_TOK
    rising = 3.0 ** (replica.astype(jnp.float32) / max(count_repl - 1, 1))
    return (values * rising[:, None]).astype(jnp.bfloat16)


def draw_norm_gain(key, part):
    key = jax.random.fold_in(key, 3)
    position = jnp.arange(D).astype(jnp.float32) / D
    base = 0.6 * 3.0 ** position
    noise = jnp.clip(1.0 + 0.12 * jax.random.normal(key, (D,), jnp.float32), 0.75, 1.25)
    return base * noise


def steps_of(key, dims, shards, smallest, high):
    level, own = 1.0, jax.random.fold_in(key, 6)
    for axis_at, parts in shards:
        heights = jnp.exp(jax.random.uniform(jax.random.fold_in(own, axis_at), (parts,), jnp.float32, smallest / len(shards), high / len(shards)))
        level = level * jnp.repeat(heights, dims[axis_at] // parts).reshape([-1 if axis == axis_at else 1 for axis in range(len(dims))])
    return level


def centred(own_key, dims, deviation, most, cuts=(), held_as=jnp.bfloat16):
    factor_of = steps_of(own_key, dims, cuts, -0.22, 0.18) if cuts else 1.0
    drawn = jax.random.normal(own_key, dims, jnp.float32) * deviation * factor_of
    return jnp.minimum(jnp.maximum(drawn, -most), most).astype(held_as)


def setup_inputs(seed: int = 0) -> dict:
    keys = jax.random.split(jax.random.key(seed), 5)
    layer_input = draw_layer_input(jax.random.fold_in(keys[4], 71), 0)
    norm_gain = draw_norm_gain(jax.random.fold_in(keys[4], 71), 0)
    value_weight = centred(keys[2], (D, W), W ** -0.5, 0.25, ((0, 16),))
    value_cotangent = draw_value_cotangent(jax.random.fold_in(keys[4], 71), 0)
    return {"layer_input": layer_input, "norm_gain": norm_gain, "value_weight": value_weight, "value_cotangent": value_cotangent}


EPS_NORM = 1e-05
EPS_SUM = 1e-06

def replica_terms(pair, norm_gain, value_weight):
    layer_input, value_cotangent = pair
    grad_scale = 1.0 / math.sqrt(REPL_TOK)
    input32 = layer_input.astype(jnp.float32)
    inverse_rms = lax.rsqrt(lax.optimization_barrier(jnp.mean(input32 * input32, axis=1, keepdims=True)) + EPS_NORM)
    normed = input32 * inverse_rms
    normed_b = lax.optimization_barrier(normed.astype(jnp.bfloat16))
    normed_bf = normed_b.astype(jnp.float32)
    scaled = (normed_bf * norm_gain[None, :]).astype(jnp.bfloat16)
    grad_w = (jnp.dot(scaled.T, value_cotangent, preferred_element_type=jnp.float32) * grad_scale).astype(jnp.bfloat16)
    back = jnp.dot(value_cotangent, value_weight.T, preferred_element_type=jnp.float32)
    grad_g = (lax.optimization_barrier(jnp.sum(back * normed_bf, axis=0)) * grad_scale).astype(jnp.bfloat16)
    hat_grad = lax.optimization_barrier((back * norm_gain[None, :]).astype(jnp.bfloat16))
    hat32 = hat_grad.astype(jnp.float32)
    mean_term = lax.optimization_barrier(jnp.mean(hat32 * normed, axis=1, keepdims=True))
    input_grad = (inverse_rms * (hat32 - normed * mean_term)).astype(jnp.bfloat16)
    return (grad_w, grad_g, input_grad)

def mix_level(vectors, pair_bit):
    partner = jnp.asarray(np.arange(N_DP) ^ 1 << pair_bit, dtype=jnp.int32)
    mine = vectors.astype(jnp.float32)
    other = jnp.take(mine, partner, axis=0)
    axes_sum = tuple(range(1, mine.ndim))
    norm_mine = lax.optimization_barrier(jnp.sum(mine * mine, axis=axes_sum))
    norm_other = lax.optimization_barrier(jnp.sum(other * other, axis=axes_sum))
    inner = lax.optimization_barrier(jnp.sum(mine * other, axis=axes_sum))
    coef_mine = 1.0 - inner / (2.0 * (norm_mine + EPS_SUM))
    coef_other = 1.0 - inner / (2.0 * (norm_other + EPS_SUM))
    shape_coef = (N_DP,) + (1,) * (mine.ndim - 1)
    return (coef_mine.reshape(shape_coef) * mine + coef_other.reshape(shape_coef) * other).astype(jnp.bfloat16)

def reference(layer_input, norm_gain, value_weight, value_cotangent):
    inputs_rep = layer_input.reshape(N_DP, REPL_TOK, D)
    cotan_rep = value_cotangent.reshape(N_DP, REPL_TOK, W)
    grad_w, grad_g, input_grad = lax.map(partial_terms(norm_gain, value_weight), (inputs_rep, cotan_rep))
    for depth_step in range(LEVELS):
        pair_bit = LEVELS - 1 - depth_step
        grad_w = mix_level(grad_w, pair_bit)
        grad_g = mix_level(grad_g, pair_bit)
    return (input_grad.reshape(TOKENS, D), grad_w[0], grad_g[0])

def partial_terms(norm_gain, value_weight):

    def apply_terms(pair):
        return replica_terms(pair, norm_gain, value_weight)
    return apply_terms
```

```python
import math

import jax
import jax.numpy as jnp
from jax import lax
from jax.experimental import pallas as pl
from jax.experimental.pallas import tpu as pltpu
from jax.sharding import PartitionSpec as P

EPS_NORM = 1e-05
EPS_SUM = 1e-06
REPLICAS = 32
LANES = 128


def pack_gram(gram):
    row = lax.broadcasted_iota(jnp.int32, gram.shape, 0)
    lane = lax.broadcasted_iota(jnp.int32, gram.shape, 1)
    kept = jnp.where(row // 8 == lane // REPLICAS, gram, 0.0)
    return kept[0:8] + kept[8:16] + kept[16:24] + kept[24:32]


def unpack_gram(packed):
    tiled = jnp.concatenate([packed] * 4, axis=0)
    row = lax.broadcasted_iota(jnp.int32, tiled.shape, 0)
    lane = lax.broadcasted_iota(jnp.int32, tiled.shape, 1)
    kept = jnp.where(row // 8 == lane // REPLICAS, tiled, 0.0)
    kept = kept + pltpu.roll(kept, 64, 1)
    return kept + pltpu.roll(kept, 32, 1)


def gram_kernel(shards_ref, gain_ref, out_ref):
    shards = shards_ref[...]
    products = lax.dot_general(
        shards, shards, (((1,), (1,)), ((), ())), preferred_element_type=jnp.float32
    )
    rows, width = products.shape[0], shards.shape[0] // REPLICAS
    row = lax.broadcasted_iota(jnp.int32, products.shape, 0)
    column = lax.broadcasted_iota(jnp.int32, products.shape, 1)
    kept = jnp.where(row % width == column % width, products, 0.0)
    folded = jnp.sum(kept.reshape(REPLICAS, width, rows), axis=1)
    source = lax.broadcasted_iota(jnp.int32, (rows, LANES), 0)
    target = lax.broadcasted_iota(jnp.int32, (rows, LANES), 1)
    spread = jnp.where(source // width == target % REPLICAS, 1.0, 0.0)
    gram = jnp.dot(
        folded, spread, precision=lax.Precision.HIGHEST, preferred_element_type=jnp.float32
    )
    packed = pack_gram(gram)
    gain = gain_ref[...]
    for peer in range(out_ref.shape[0]):
        out_ref[peer, 0:8, :] = packed
        for part in range(4):
            out_ref[peer, 8 + part : 9 + part, :] = gain[:, part * LANES : (part + 1) * LANES]
        out_ref[peer, 12:16, :] = jnp.zeros((4, LANES), jnp.float32)


def gain_gram_kernel(parts_ref, out_ref):
    packed = jnp.sum(parts_ref[:, 0:8, :], axis=0)
    gram = jnp.zeros((REPLICAS, REPLICAS), jnp.float32)
    for part in range(4):
        piece = parts_ref[:, 8 + part, :].astype(jnp.bfloat16)
        gram += lax.dot_general(
            piece, piece, (((1,), (1,)), ((), ())), preferred_element_type=jnp.float32
        )
    packed_gain = pack_gram(jnp.concatenate([gram] * 4, axis=1))
    for peer in range(out_ref.shape[0]):
        out_ref[peer, 0:8, :] = packed
        out_ref[peer, 8:16, :] = packed_gain


def swap(values, stride, axis):
    size = values.shape[axis]
    index = lax.broadcasted_iota(jnp.int32, values.shape, axis)
    up = pltpu.roll(values, size - stride, axis)
    down = pltpu.roll(values, stride, axis)
    return jnp.where((index & stride) == 0, up, down)


def pair_weights(gram):
    row = lax.broadcasted_iota(jnp.int32, gram.shape, 0)
    lane = lax.broadcasted_iota(jnp.int32, gram.shape, 1)
    column = lane % REPLICAS
    first = lane < REPLICAS
    weights = jnp.ones((REPLICAS, 1), jnp.float32)
    for stride in (16, 8, 4, 2, 1):
        same = row == column
        met = row == (column ^ stride)

        def coefs(axis, only):
            norm = jnp.sum(jnp.where(same & only, gram, 0.0), axis=axis, keepdims=True)
            inner = jnp.sum(jnp.where(met & only, gram, 0.0), axis=axis, keepdims=True)
            return 1.0 - inner / (2.0 * (jnp.maximum(norm, 0.0) + EPS_SUM))

        down = coefs(1, first)
        weights = weights * down
        if stride > 1:
            scaled = gram * down * coefs(0, True)
            scaled = scaled + swap(scaled, stride, 0)
            gram = scaled + swap(scaled, stride, 1)
    return weights


def combine_kernel(packed_ref, shards_ref, parts_ref, weight_ref, gain_ref):
    packed = jnp.sum(packed_ref[...], axis=0)
    weights_w = pair_weights(unpack_gram(packed[0:8]))
    weights_g = pair_weights(unpack_gram(packed[8:16]))
    width = shards_ref.shape[0] // REPLICAS
    total = jnp.zeros((width, shards_ref.shape[1]), jnp.float32)
    for replica in range(REPLICAS):
        shard = shards_ref[replica * width : (replica + 1) * width, :].astype(jnp.float32)
        total += weights_w[replica : replica + 1, :] * shard
    weight_ref[...] = total.T.astype(jnp.bfloat16)
    for part in range(4):
        piece = parts_ref[:, 8 + part, :]
        gain_ref[:, part * LANES : (part + 1) * LANES] = jnp.sum(
            weights_g * piece, axis=0, keepdims=True
        ).astype(jnp.bfloat16)


def kernel_call(kernel, out_shape, *args):
    return pl.pallas_call(
        kernel,
        out_shape=out_shape,
        compiler_params=pltpu.CompilerParams(vmem_limit_bytes=32 * 1024 * 1024),
    )(*args)


def body(layer_input, norm_gain, value_weight, value_cotangent):
    tokens, model = layer_input.shape
    peers = lax.axis_size("fsdp")
    columns = lax.all_to_all(layer_input, "fsdp", split_axis=1, concat_axis=0, tiled=True)
    input32 = layer_input.astype(jnp.float32)
    inverse_rms = lax.rsqrt(jnp.mean(input32 * input32, axis=1, keepdims=True) + EPS_NORM)
    scaled_cotangent = (value_cotangent.astype(jnp.float32) * inverse_rms).astype(jnp.bfloat16)
    cotangent = lax.all_gather(scaled_cotangent, "fsdp", axis=0, tiled=True)
    grad_scale = 1.0 / math.sqrt(cotangent.shape[0])
    grad = lax.dot_general(
        cotangent, columns, (((0,), (0,)), ((), ())), preferred_element_type=jnp.float32
    )
    grad_w = (grad * (norm_gain * grad_scale)[None, :]).astype(jnp.bfloat16)
    weight_t = value_weight.T.astype(jnp.float32)
    grad_g = (jnp.sum(grad * weight_t, axis=0, keepdims=True) * grad_scale).astype(jnp.bfloat16)
    back = lax.dot_general(
        cotangent, value_weight, (((1,), (1,)), ((), ())), preferred_element_type=jnp.float32
    )
    hat_grad = (back * norm_gain[None, :]).astype(jnp.bfloat16)
    shards = lax.all_to_all(grad_w, "dp", split_axis=0, concat_axis=0, tiled=True)
    returned = lax.all_to_all(hat_grad, "fsdp", split_axis=0, concat_axis=1, tiled=True)

    sent = kernel_call(
        gram_kernel,
        jax.ShapeDtypeStruct((REPLICAS, 16, LANES), jnp.float32),
        shards,
        grad_g.astype(jnp.float32),
    )
    parts = lax.all_to_all(sent, "dp", split_axis=0, concat_axis=0, tiled=True)
    sent = kernel_call(
        gain_gram_kernel, jax.ShapeDtypeStruct((peers, 16, LANES), jnp.float32), parts
    )
    packed = lax.all_to_all(sent, "fsdp", split_axis=0, concat_axis=0, tiled=True)
    weight_update, gain_update = kernel_call(
        combine_kernel,
        (
            jax.ShapeDtypeStruct((shards.shape[1], shards.shape[0] // REPLICAS), jnp.bfloat16),
            jax.ShapeDtypeStruct((1, shards.shape[1]), jnp.bfloat16),
        ),
        packed,
        shards,
        parts,
    )
    hat32 = returned.astype(jnp.float32)
    mean_term = jnp.mean(hat32 * input32, axis=1, keepdims=True)
    input_grad = (hat32 - input32 * (inverse_rms * inverse_rms * mean_term)).astype(jnp.bfloat16)
    return (input_grad, weight_update, gain_update[0])


def solution(mesh):
    in_specs = (P(("dp", "fsdp"), None), P("fsdp"), P("fsdp", None), P(("dp", "fsdp"), None))
    out_specs = (P(("dp", "fsdp"), None), P("fsdp", "dp"), P("fsdp"))
    return jax.shard_map(body, mesh=mesh, in_specs=in_specs, out_specs=out_specs, check_vma=False)
```

```python
import math

import jax
import jax.numpy as jnp
from jax import lax
from jax.experimental import pallas as pl
from jax.experimental.pallas import tpu as pltpu
from jax.sharding import PartitionSpec as P

EPS_NORM = 1e-05
EPS_SUM = 1e-06
REPLICAS = 32
LANES = 128
PARAMS = pltpu.CompilerParams(vmem_limit_bytes=32 * 1024 * 1024)


def pack_gram(gram):
    row = lax.broadcasted_iota(jnp.int32, gram.shape, 0)
    lane = lax.broadcasted_iota(jnp.int32, gram.shape, 1)
    kept = jnp.where(row // 8 == lane // REPLICAS, gram, 0.0)
    return kept[0:8] + kept[8:16] + kept[16:24] + kept[24:32]


def unpack_gram(packed):
    tiled = jnp.concatenate([packed] * 4, axis=0)
    row = lax.broadcasted_iota(jnp.int32, tiled.shape, 0)
    lane = lax.broadcasted_iota(jnp.int32, tiled.shape, 1)
    kept = jnp.where(row // 8 == lane // REPLICAS, tiled, 0.0)
    kept = kept + pltpu.roll(kept, 64, 1)
    return kept + pltpu.roll(kept, 32, 1)


def gram_kernel(shards_ref, gain_ref, out_ref):
    shards = shards_ref[...]
    products = lax.dot_general(
        shards, shards, (((1,), (1,)), ((), ())), preferred_element_type=jnp.float32
    )
    rows, width = products.shape[0], shards.shape[0] // REPLICAS
    row = lax.broadcasted_iota(jnp.int32, products.shape, 0)
    column = lax.broadcasted_iota(jnp.int32, products.shape, 1)
    kept = jnp.where(row % width == column % width, products, 0.0)
    folded = jnp.sum(kept.reshape(REPLICAS, width, rows), axis=1)
    source = lax.broadcasted_iota(jnp.int32, (rows, LANES), 0)
    target = lax.broadcasted_iota(jnp.int32, (rows, LANES), 1)
    spread = jnp.where(source // width == target % REPLICAS, 1.0, 0.0)
    gram = jnp.dot(
        folded, spread, precision=lax.Precision.HIGHEST, preferred_element_type=jnp.float32
    )
    packed = pack_gram(gram)
    gain = gain_ref[...]
    for peer in range(out_ref.shape[0]):
        out_ref[peer, 0:8, :] = packed
        for part in range(4):
            out_ref[peer, 8 + part : 9 + part, :] = gain[:, part * LANES : (part + 1) * LANES]
        out_ref[peer, 12:16, :] = jnp.zeros((4, LANES), jnp.float32)


def gain_gram_kernel(parts_ref, out_ref):
    packed = jnp.sum(parts_ref[:, 0:8, :], axis=0)
    gram = jnp.zeros((REPLICAS, REPLICAS), jnp.float32)
    for part in range(4):
        piece = parts_ref[:, 8 + part, :].astype(jnp.bfloat16)
        gram += lax.dot_general(
            piece, piece, (((1,), (1,)), ((), ())), preferred_element_type=jnp.float32
        )
    packed_gain = pack_gram(jnp.concatenate([gram] * 4, axis=1))
    for peer in range(out_ref.shape[0]):
        out_ref[peer, 0:8, :] = packed
        out_ref[peer, 8:16, :] = packed_gain


def swap(values, stride, axis):
    size = values.shape[axis]
    index = lax.broadcasted_iota(jnp.int32, values.shape, axis)
    up = pltpu.roll(values, size - stride, axis)
    down = pltpu.roll(values, stride, axis)
    return jnp.where((index & stride) == 0, up, down)


def pair_weights(gram):
    row = lax.broadcasted_iota(jnp.int32, gram.shape, 0)
    lane = lax.broadcasted_iota(jnp.int32, gram.shape, 1)
    column = lane % REPLICAS
    first = lane < REPLICAS
    weights = jnp.ones((REPLICAS, 1), jnp.float32)
    for stride in (16, 8, 4, 2, 1):
        same = row == column
        met = row == (column ^ stride)

        def coefs(axis, only):
            norm = jnp.sum(jnp.where(same & only, gram, 0.0), axis=axis, keepdims=True)
            inner = jnp.sum(jnp.where(met & only, gram, 0.0), axis=axis, keepdims=True)
            return 1.0 - inner / (2.0 * (jnp.maximum(norm, 0.0) + EPS_SUM))

        down = coefs(1, first)
        weights = weights * down
        if stride > 1:
            scaled = gram * down * coefs(0, True)
            scaled = scaled + swap(scaled, stride, 0)
            gram = scaled + swap(scaled, stride, 1)
    return weights


def combine_kernel(packed_ref, shards_ref, parts_ref, weight_ref, gain_ref):
    packed = jnp.sum(packed_ref[...], axis=0)
    weights_w = pair_weights(unpack_gram(packed[0:8]))
    weights_g = pair_weights(unpack_gram(packed[8:16]))
    width = shards_ref.shape[0] // REPLICAS
    total = jnp.zeros((width, shards_ref.shape[1]), jnp.float32)
    for replica in range(REPLICAS):
        shard = shards_ref[replica * width : (replica + 1) * width, :].astype(jnp.float32)
        total += weights_w[replica : replica + 1, :] * shard
    weight_ref[...] = total.astype(jnp.bfloat16)
    for part in range(4):
        piece = parts_ref[:, 8 + part, :]
        gain_ref[:, part * LANES : (part + 1) * LANES] = jnp.sum(
            weights_g * piece, axis=0, keepdims=True
        ).astype(jnp.bfloat16)


def kernel_call(kernel, out_shape, *args):
    return pl.pallas_call(
        kernel,
        out_shape=out_shape,
        compiler_params=PARAMS,
    )(*args)


def norm_kernel(input_ref, blocks_ref):
    input32 = input_ref[...].astype(jnp.float32)
    square = jnp.mean(input32 * input32, axis=1, keepdims=True)
    normed = (input32 * lax.rsqrt(square + EPS_NORM)).astype(jnp.bfloat16)
    width = blocks_ref.shape[2]
    for owner in range(blocks_ref.shape[0]):
        blocks_ref[owner, :, :] = normed[:, owner * width : (owner + 1) * width]


def input_kernel(input_ref, cotangent_ref, weight_ref, out_ref, hat_ref, total_ref):
    step, steps = pl.program_id(0), pl.num_programs(0)
    width = weight_ref.shape[0]

    @pl.when(step == 0)
    def _():
        total_ref[...] = jnp.zeros_like(total_ref)

    hat = lax.dot_general(
        cotangent_ref[...],
        weight_ref[...],
        (((1,), (1,)), ((), ())),
        preferred_element_type=jnp.float32,
    ).astype(jnp.bfloat16)
    columns = pl.ds(pl.multiple_of(step * width, width), width)
    hat_ref[:, columns] = hat
    total_ref[...] += hat.astype(jnp.float32) * input_ref[:, columns].astype(jnp.float32)

    @pl.when(step == steps - 1)
    def _():
        model = input_ref.shape[1]
        square = jnp.zeros_like(total_ref)
        for part in range(model // width):
            piece = input_ref[:, part * width : (part + 1) * width].astype(jnp.float32)
            square += piece * piece
        inverse_rms = lax.rsqrt(jnp.sum(square, axis=1, keepdims=True) / model + EPS_NORM)
        mean_term = jnp.sum(total_ref[...], axis=1, keepdims=True) / model * inverse_rms
        factor = inverse_rms * mean_term
        for part in range(model // width):
            at = slice(part * width, (part + 1) * width)
            piece = input_ref[:, at].astype(jnp.float32)
            out_ref[:, at] = (
                inverse_rms * (hat_ref[:, at].astype(jnp.float32) - piece * factor)
            ).astype(jnp.bfloat16)


def body(layer_input, norm_gain, value_weight, value_cotangent):
    tokens, model = layer_input.shape
    peers, width = lax.axis_size("fsdp"), value_cotangent.shape[1]
    own = model // peers
    cotangent = lax.all_gather(value_cotangent, "fsdp", axis=0, tiled=True)
    step = 16
    blocks = pl.pallas_call(
        norm_kernel,
        grid=(tokens // step,),
        in_specs=[pl.BlockSpec((step, model), lambda i: (i, 0))],
        out_specs=pl.BlockSpec((peers, step, own), lambda i: (0, i, 0)),
        out_shape=jax.ShapeDtypeStruct((peers, tokens, own), jnp.bfloat16),
        compiler_params=PARAMS,
    )(layer_input)
    columns = lax.all_to_all(blocks, "fsdp", split_axis=0, concat_axis=0, tiled=True)
    columns = columns.reshape(peers * tokens, own)
    scaled_weight = (value_weight.astype(jnp.float32) * norm_gain[:, None]).astype(jnp.bfloat16)
    scaled_weight, cotangent = lax.optimization_barrier((scaled_weight, cotangent))
    all_weight = lax.all_gather(scaled_weight, "fsdp", axis=0, tiled=True)

    grad_scale = 1.0 / math.sqrt(cotangent.shape[0])
    grad = lax.dot_general(
        cotangent, columns, (((0,), (0,)), ((), ())), preferred_element_type=jnp.float32
    )
    grad_w = (grad * (norm_gain * grad_scale)[None, :]).astype(jnp.bfloat16)
    weight_t = value_weight.T.astype(jnp.float32)
    grad_g = (jnp.sum(grad * weight_t, axis=0, keepdims=True) * grad_scale).astype(jnp.bfloat16)
    shards = lax.all_to_all(grad_w, "dp", split_axis=0, concat_axis=0, tiled=True)

    sent = kernel_call(
        gram_kernel,
        jax.ShapeDtypeStruct((REPLICAS, 16, LANES), jnp.float32),
        shards,
        grad_g.astype(jnp.float32),
    )
    parts = lax.all_to_all(sent, "dp", split_axis=0, concat_axis=0, tiled=True)
    sent = kernel_call(
        gain_gram_kernel, jax.ShapeDtypeStruct((peers, 16, LANES), jnp.float32), parts
    )
    packed = lax.all_to_all(sent, "fsdp", split_axis=0, concat_axis=0, tiled=True)
    weight_update, gain_update = kernel_call(
        combine_kernel,
        (
            jax.ShapeDtypeStruct((shards.shape[0] // REPLICAS, own), jnp.bfloat16),
            jax.ShapeDtypeStruct((1, own), jnp.bfloat16),
        ),
        packed,
        shards,
        parts,
    )
    input_grad = pl.pallas_call(
        input_kernel,
        grid=(peers,),
        in_specs=[
            pl.BlockSpec((tokens, model), lambda i: (0, 0)),
            pl.BlockSpec((tokens, width), lambda i: (0, 0)),
            pl.BlockSpec((own, width), lambda i: (i, 0)),
        ],
        out_specs=pl.BlockSpec((tokens, model), lambda i: (0, 0)),
        out_shape=jax.ShapeDtypeStruct((tokens, model), jnp.bfloat16),
        scratch_shapes=[
            pltpu.VMEM((tokens, model), jnp.bfloat16),
            pltpu.VMEM((tokens, own), jnp.float32),
        ],
        compiler_params=PARAMS,
        cost_estimate=pl.CostEstimate(
            flops=2 * tokens * model * width, bytes_accessed=2 * model * (width + 2 * tokens), transcendentals=0
        ),
    )(layer_input, value_cotangent, all_weight)
    return (input_grad, weight_update.T, gain_update[0])


def solution(mesh):
    in_specs = (P(("dp", "fsdp"), None), P("fsdp"), P("fsdp", None), P(("dp", "fsdp"), None))
    out_specs = (P(("dp", "fsdp"), None), P("fsdp", "dp"), P("fsdp"))
    return jax.shard_map(body, mesh=mesh, in_specs=in_specs, out_specs=out_specs, check_vma=False)
```

```python
import math

import jax
import jax.numpy as jnp
from jax import lax
from jax.experimental import pallas as pl
from jax.experimental.pallas import tpu as pltpu
from jax.sharding import PartitionSpec as P

EPS_NORM = 1e-05
EPS_SUM = 1e-06
REPLICAS = 32
LANES = 128
PARAMS = pltpu.CompilerParams(vmem_limit_bytes=32 * 1024 * 1024)
LARGE = pltpu.CompilerParams(vmem_limit_bytes=60 * 1024 * 1024)


def pack_gram(gram):
    row = lax.broadcasted_iota(jnp.int32, gram.shape, 0)
    lane = lax.broadcasted_iota(jnp.int32, gram.shape, 1)
    kept = jnp.where(row // 8 == lane // REPLICAS, gram, 0.0)
    return kept[0:8] + kept[8:16] + kept[16:24] + kept[24:32]


def unpack_gram(packed):
    tiled = jnp.concatenate([packed] * 4, axis=0)
    row = lax.broadcasted_iota(jnp.int32, tiled.shape, 0)
    lane = lax.broadcasted_iota(jnp.int32, tiled.shape, 1)
    kept = jnp.where(row // 8 == lane // REPLICAS, tiled, 0.0)
    kept = kept + pltpu.roll(kept, 64, 1)
    return kept + pltpu.roll(kept, 32, 1)


def gram_kernel(shards_ref, gain_ref, out_ref):
    shards = shards_ref[...]
    products = lax.dot_general(
        shards, shards, (((1,), (1,)), ((), ())), preferred_element_type=jnp.float32
    )
    rows, width = products.shape[0], shards.shape[0] // REPLICAS
    row = lax.broadcasted_iota(jnp.int32, products.shape, 0)
    column = lax.broadcasted_iota(jnp.int32, products.shape, 1)
    kept = jnp.where(row % width == column % width, products, 0.0)
    folded = jnp.sum(kept.reshape(REPLICAS, width, rows), axis=1)
    source = lax.broadcasted_iota(jnp.int32, (rows, LANES), 0)
    target = lax.broadcasted_iota(jnp.int32, (rows, LANES), 1)
    spread = jnp.where(source // width == target % REPLICAS, 1.0, 0.0)
    gram = jnp.dot(
        folded, spread, precision=lax.Precision.HIGHEST, preferred_element_type=jnp.float32
    )
    packed = pack_gram(gram)
    gain = gain_ref[...]
    for peer in range(out_ref.shape[0]):
        out_ref[peer, 0:8, :] = packed
        for part in range(4):
            out_ref[peer, 8 + part : 9 + part, :] = gain[:, part * LANES : (part + 1) * LANES]
        out_ref[peer, 12:16, :] = jnp.zeros((4, LANES), jnp.float32)


def gain_gram_kernel(parts_ref, out_ref):
    packed = jnp.sum(parts_ref[:, 0:8, :], axis=0)
    gram = jnp.zeros((REPLICAS, REPLICAS), jnp.float32)
    for part in range(4):
        piece = parts_ref[:, 8 + part, :].astype(jnp.bfloat16)
        gram += lax.dot_general(
            piece, piece, (((1,), (1,)), ((), ())), preferred_element_type=jnp.float32
        )
    packed_gain = pack_gram(jnp.concatenate([gram] * 4, axis=1))
    for peer in range(out_ref.shape[0]):
        out_ref[peer, 0:8, :] = packed
        out_ref[peer, 8:16, :] = packed_gain


def swap(values, stride, axis):
    size = values.shape[axis]
    index = lax.broadcasted_iota(jnp.int32, values.shape, axis)
    up = pltpu.roll(values, size - stride, axis)
    down = pltpu.roll(values, stride, axis)
    return jnp.where((index & stride) == 0, up, down)


def pair_weights(gram):
    row = lax.broadcasted_iota(jnp.int32, gram.shape, 0)
    lane = lax.broadcasted_iota(jnp.int32, gram.shape, 1)
    column = lane % REPLICAS
    first = lane < REPLICAS
    weights = jnp.ones((REPLICAS, 1), jnp.float32)
    for stride in (16, 8, 4, 2, 1):
        same = row == column
        met = row == (column ^ stride)

        def coefs(axis, only):
            norm = jnp.sum(jnp.where(same & only, gram, 0.0), axis=axis, keepdims=True)
            inner = jnp.sum(jnp.where(met & only, gram, 0.0), axis=axis, keepdims=True)
            return 1.0 - inner / (2.0 * (jnp.maximum(norm, 0.0) + EPS_SUM))

        down = coefs(1, first)
        weights = weights * down
        if stride > 1:
            scaled = gram * down * coefs(0, True)
            scaled = scaled + swap(scaled, stride, 0)
            gram = scaled + swap(scaled, stride, 1)
    return weights


def combine_kernel(packed_ref, shards_ref, parts_ref, weight_ref, gain_ref):
    packed = jnp.sum(packed_ref[...], axis=0)
    weights_w = pair_weights(unpack_gram(packed[0:8]))
    weights_g = pair_weights(unpack_gram(packed[8:16]))
    width = shards_ref.shape[0] // REPLICAS
    total = jnp.zeros((width, shards_ref.shape[1]), jnp.float32)
    for replica in range(REPLICAS):
        shard = shards_ref[replica * width : (replica + 1) * width, :].astype(jnp.float32)
        total += weights_w[replica : replica + 1, :] * shard
    weight_ref[...] = total.astype(jnp.bfloat16)
    for part in range(4):
        piece = parts_ref[:, 8 + part, :]
        gain_ref[:, part * LANES : (part + 1) * LANES] = jnp.sum(
            weights_g * piece, axis=0, keepdims=True
        ).astype(jnp.bfloat16)


def kernel_call(kernel, out_shape, *args):
    return pl.pallas_call(
        kernel,
        out_shape=out_shape,
        compiler_params=PARAMS,
    )(*args)


def norm_kernel(input_ref, blocks_ref, scale_ref):
    input32 = input_ref[...].astype(jnp.float32)
    square = jnp.mean(input32 * input32, axis=1, keepdims=True)
    inverse_rms = lax.rsqrt(square + EPS_NORM)
    scale_ref[...] = jnp.broadcast_to(inverse_rms, scale_ref.shape)
    normed = (input32 * inverse_rms).astype(jnp.bfloat16)
    width = blocks_ref.shape[2]
    for owner in range(blocks_ref.shape[0]):
        blocks_ref[owner, :, :] = normed[:, owner * width : (owner + 1) * width]


def input_kernel(input_ref, cotangent_ref, weight_ref, scale_ref, out_ref, hat_ref, total_ref):
    step, steps = pl.program_id(0), pl.num_programs(0)
    model, width = input_ref.shape[1], weight_ref.shape[2]

    @pl.when(step == 0)
    def _():
        total_ref[...] = jnp.zeros_like(total_ref)

    for block in range(weight_ref.shape[0]):
        hat = jnp.dot(
            cotangent_ref[...], weight_ref[block], preferred_element_type=jnp.float32
        ).astype(jnp.bfloat16)
        at = (step * weight_ref.shape[0] + block) * width
        columns = pl.ds(pl.multiple_of(at, width), width)
        hat_ref[:, columns] = hat
        total_ref[...] += hat.astype(jnp.float32) * input_ref[:, columns].astype(jnp.float32)

    @pl.when(step == steps - 1)
    def _():
        inverse_rms = scale_ref[:, 0:1]
        factor = jnp.sum(total_ref[...], axis=1, keepdims=True) / model
        factor = inverse_rms * inverse_rms * factor
        for part in range(model // width):
            at = slice(part * width, (part + 1) * width)
            piece = input_ref[:, at].astype(jnp.float32)
            out_ref[:, at] = (
                inverse_rms * (hat_ref[:, at].astype(jnp.float32) - piece * factor)
            ).astype(jnp.bfloat16)


def body(layer_input, norm_gain, value_weight, value_cotangent):
    tokens, model = layer_input.shape
    peers, width = lax.axis_size("fsdp"), value_cotangent.shape[1]
    own = model // peers
    cotangent = lax.all_gather(value_cotangent, "fsdp", axis=0, tiled=True)
    step = 32
    blocks, scale = pl.pallas_call(
        norm_kernel,
        grid=(tokens // step,),
        in_specs=[pl.BlockSpec((step, model), lambda i: (i, 0))],
        out_specs=(
            pl.BlockSpec((peers, step, own), lambda i: (0, i, 0)),
            pl.BlockSpec((step, LANES), lambda i: (i, 0)),
        ),
        out_shape=(
            jax.ShapeDtypeStruct((peers, tokens, own), jnp.bfloat16),
            jax.ShapeDtypeStruct((tokens, LANES), jnp.float32),
        ),
        compiler_params=LARGE,
    )(layer_input)
    columns = lax.all_to_all(blocks, "fsdp", split_axis=0, concat_axis=0, tiled=True)
    columns = columns.reshape(peers * tokens, own)
    weight_t = value_weight.T.astype(jnp.float32)
    scaled_weight = (weight_t * norm_gain[None, :]).astype(jnp.bfloat16)
    scaled_weight, columns = lax.optimization_barrier((scaled_weight, columns))
    all_weight = lax.all_gather(scaled_weight, "fsdp", axis=0)

    grad_scale = 1.0 / math.sqrt(cotangent.shape[0])
    grad = lax.dot_general(
        cotangent, columns, (((0,), (0,)), ((), ())), preferred_element_type=jnp.float32
    )
    grad_w = (grad * (norm_gain * grad_scale)[None, :]).astype(jnp.bfloat16)
    grad_g = (jnp.sum(grad * weight_t, axis=0, keepdims=True) * grad_scale).astype(jnp.bfloat16)
    shards = lax.all_to_all(grad_w, "dp", split_axis=0, concat_axis=0, tiled=True)

    sent = kernel_call(
        gram_kernel,
        jax.ShapeDtypeStruct((REPLICAS, 16, LANES), jnp.float32),
        shards,
        grad_g.astype(jnp.float32),
    )
    parts = lax.all_to_all(sent, "dp", split_axis=0, concat_axis=0, tiled=True)
    sent = kernel_call(
        gain_gram_kernel, jax.ShapeDtypeStruct((peers, 16, LANES), jnp.float32), parts
    )
    packed = lax.all_to_all(sent, "fsdp", split_axis=0, concat_axis=0, tiled=True)
    weight_update, gain_update = kernel_call(
        combine_kernel,
        (
            jax.ShapeDtypeStruct((shards.shape[0] // REPLICAS, own), jnp.bfloat16),
            jax.ShapeDtypeStruct((1, own), jnp.bfloat16),
        ),
        packed,
        shards,
        parts,
    )
    group = 4
    input_grad = pl.pallas_call(
        input_kernel,
        grid=(peers // group,),
        in_specs=[
            pl.BlockSpec((tokens, model), lambda i: (0, 0)),
            pl.BlockSpec((tokens, width), lambda i: (0, 0)),
            pl.BlockSpec((group, width, own), lambda i: (i, 0, 0)),
            pl.BlockSpec((tokens, LANES), lambda i: (0, 0)),
        ],
        out_specs=pl.BlockSpec((tokens, model), lambda i: (0, 0)),
        out_shape=jax.ShapeDtypeStruct((tokens, model), jnp.bfloat16),
        scratch_shapes=[
            pltpu.VMEM((tokens, model), jnp.bfloat16),
            pltpu.VMEM((tokens, own), jnp.float32),
        ],
        compiler_params=LARGE,
        cost_estimate=pl.CostEstimate(
            flops=2 * tokens * model * width, bytes_accessed=2 * model * (width + 2 * tokens), transcendentals=0
        ),
    )(layer_input, value_cotangent, all_weight, scale)
    return (input_grad, weight_update.T, gain_update[0])


def solution(mesh):
    in_specs = (P(("dp", "fsdp"), None), P("fsdp"), P("fsdp", None), P(("dp", "fsdp"), None))
    out_specs = (P(("dp", "fsdp"), None), P("fsdp", "dp"), P("fsdp"))
    return jax.shard_map(body, mesh=mesh, in_specs=in_specs, out_specs=out_specs, check_vma=False)
```

```python
import math

import jax
import jax.numpy as jnp
from jax import lax
from jax.experimental import pallas as pl
from jax.experimental.pallas import tpu as pltpu
from jax.sharding import PartitionSpec as P

EPS_NORM = 1e-05
EPS_SUM = 1e-06
REPLICAS = 32
LANES = 128
PARAMS = pltpu.CompilerParams(vmem_limit_bytes=32 * 1024 * 1024)
INPUT = pltpu.CompilerParams(vmem_limit_bytes=57 * 1024 * 1024)
LARGE = pltpu.CompilerParams(vmem_limit_bytes=60 * 1024 * 1024)


def pack_gram(gram):
    row = lax.broadcasted_iota(jnp.int32, gram.shape, 0)
    lane = lax.broadcasted_iota(jnp.int32, gram.shape, 1)
    kept = jnp.where(row // 8 == lane // REPLICAS, gram, 0.0)
    return kept[0:8] + kept[8:16] + kept[16:24] + kept[24:32]


def unpack_gram(packed):
    tiled = jnp.concatenate([packed] * 4, axis=0)
    row = lax.broadcasted_iota(jnp.int32, tiled.shape, 0)
    lane = lax.broadcasted_iota(jnp.int32, tiled.shape, 1)
    kept = jnp.where(row // 8 == lane // REPLICAS, tiled, 0.0)
    kept = kept + pltpu.roll(kept, 64, 1)
    return kept + pltpu.roll(kept, 32, 1)


def gram_kernel(shards_ref, gain_ref, out_ref):
    shards = shards_ref[...]
    products = lax.dot_general(
        shards, shards, (((1,), (1,)), ((), ())), preferred_element_type=jnp.float32
    )
    rows, width = products.shape[0], shards.shape[0] // REPLICAS
    row = lax.broadcasted_iota(jnp.int32, products.shape, 0)
    column = lax.broadcasted_iota(jnp.int32, products.shape, 1)
    kept = jnp.where(row % width == column % width, products, 0.0)
    folded = jnp.sum(kept.reshape(REPLICAS, width, rows), axis=1)
    source = lax.broadcasted_iota(jnp.int32, (rows, LANES), 0)
    target = lax.broadcasted_iota(jnp.int32, (rows, LANES), 1)
    spread = jnp.where(source // width == target % REPLICAS, 1.0, 0.0)
    gram = jnp.dot(
        folded, spread, precision=lax.Precision.HIGHEST, preferred_element_type=jnp.float32
    )
    packed = pack_gram(gram)
    gain = gain_ref[...]
    for peer in range(out_ref.shape[0]):
        out_ref[peer, 0:8, :] = packed
        for part in range(4):
            out_ref[peer, 8 + part : 9 + part, :] = gain[:, part * LANES : (part + 1) * LANES]
        out_ref[peer, 12:16, :] = jnp.zeros((4, LANES), jnp.float32)


def gain_gram_kernel(parts_ref, out_ref):
    packed = jnp.sum(parts_ref[:, 0:8, :], axis=0)
    gram = jnp.zeros((REPLICAS, REPLICAS), jnp.float32)
    for part in range(4):
        piece = parts_ref[:, 8 + part, :].astype(jnp.bfloat16)
        gram += lax.dot_general(
            piece, piece, (((1,), (1,)), ((), ())), preferred_element_type=jnp.float32
        )
    packed_gain = pack_gram(jnp.concatenate([gram] * 4, axis=1))
    for peer in range(out_ref.shape[0]):
        out_ref[peer, 0:8, :] = packed
        out_ref[peer, 8:16, :] = packed_gain


def swap(values, stride, axis):
    size = values.shape[axis]
    index = lax.broadcasted_iota(jnp.int32, values.shape, axis)
    up = pltpu.roll(values, size - stride, axis)
    down = pltpu.roll(values, stride, axis)
    return jnp.where((index & stride) == 0, up, down)


def pair_weights(gram):
    row = lax.broadcasted_iota(jnp.int32, gram.shape, 0)
    lane = lax.broadcasted_iota(jnp.int32, gram.shape, 1)
    column = lane % REPLICAS
    first = lane < REPLICAS
    weights = jnp.ones((REPLICAS, 1), jnp.float32)
    for stride in (16, 8, 4, 2, 1):
        same = row == column
        met = row == (column ^ stride)

        def coefs(axis, only):
            norm = jnp.sum(jnp.where(same & only, gram, 0.0), axis=axis, keepdims=True)
            inner = jnp.sum(jnp.where(met & only, gram, 0.0), axis=axis, keepdims=True)
            return 1.0 - inner / (2.0 * (jnp.maximum(norm, 0.0) + EPS_SUM))

        down = coefs(1, first)
        weights = weights * down
        if stride > 1:
            scaled = gram * down * coefs(0, True)
            scaled = scaled + swap(scaled, stride, 0)
            gram = scaled + swap(scaled, stride, 1)
    return weights


def combine_kernel(packed_ref, shards_ref, parts_ref, done_ref, weight_ref, gain_ref):
    packed = jnp.sum(packed_ref[...], axis=0)
    weights_w = pair_weights(unpack_gram(packed[0:8]))
    weights_g = pair_weights(unpack_gram(packed[8:16]))
    width = shards_ref.shape[0] // REPLICAS
    total = jnp.zeros((width, shards_ref.shape[1]), jnp.float32)
    for replica in range(REPLICAS):
        shard = shards_ref[replica * width : (replica + 1) * width, :].astype(jnp.float32)
        total += weights_w[replica : replica + 1, :] * shard
    weight_ref[...] = total.astype(jnp.bfloat16)
    gains = [
        jnp.sum(weights_g * parts_ref[:, 8 + part, :], axis=0, keepdims=True) for part in range(4)
    ]
    gain_ref[...] = jnp.concatenate(gains, axis=1)[0].astype(jnp.bfloat16)


def kernel_call(kernel, out_shape, *args):
    return pl.pallas_call(
        kernel,
        out_shape=out_shape,
        compiler_params=PARAMS,
    )(*args)


def norm_kernel(input_ref, blocks_ref, scale_ref):
    input32 = input_ref[...].astype(jnp.float32)
    square = jnp.mean(input32 * input32, axis=1, keepdims=True)
    inverse_rms = lax.rsqrt(square + EPS_NORM)
    scale_ref[...] = jnp.broadcast_to(inverse_rms, scale_ref.shape)
    normed = (input32 * inverse_rms).astype(jnp.bfloat16)
    width = blocks_ref.shape[2]
    for owner in range(blocks_ref.shape[0]):
        blocks_ref[owner, :, :] = normed[:, owner * width : (owner + 1) * width]


def input_kernel(input_ref, cotangent_ref, weight_ref, scale_ref, out_ref, done_ref, hat_ref, total_ref):
    step, steps = pl.program_id(0), pl.num_programs(0)
    model, width = input_ref.shape[1], weight_ref.shape[2]

    @pl.when(step == 0)
    def _():
        total_ref[...] = jnp.zeros_like(total_ref)
        done_ref[...] = jnp.zeros_like(done_ref)

    for block in range(weight_ref.shape[0]):
        hat = jnp.dot(
            cotangent_ref[...], weight_ref[block], preferred_element_type=jnp.float32
        ).astype(jnp.bfloat16)
        at = (step * weight_ref.shape[0] + block) * width
        columns = pl.ds(pl.multiple_of(at, width), width)
        hat_ref[:, columns] = hat
        total_ref[...] += hat.astype(jnp.float32) * input_ref[:, columns].astype(jnp.float32)

    @pl.when(step == steps - 1)
    def _():
        inverse_rms = scale_ref[:, 0:1]
        factor = jnp.sum(total_ref[...], axis=1, keepdims=True) / model
        factor = inverse_rms * inverse_rms * factor
        for part in range(model // width):
            at = slice(part * width, (part + 1) * width)
            piece = input_ref[:, at].astype(jnp.float32)
            out_ref[:, at] = (
                inverse_rms * (hat_ref[:, at].astype(jnp.float32) - piece * factor)
            ).astype(jnp.bfloat16)


def scale_kernel(weight_ref, gain_ref, cotangent_ref, out_ref):
    out_ref[...] = (weight_ref[...].T.astype(jnp.float32) * gain_ref[...]).astype(jnp.bfloat16)


def body(layer_input, norm_gain, value_weight, value_cotangent):
    tokens, model = layer_input.shape
    peers, width = lax.axis_size("fsdp"), value_cotangent.shape[1]
    own = model // peers
    cotangent = lax.all_gather(value_cotangent, "fsdp", axis=0, tiled=True)
    step = 64
    blocks, scale = pl.pallas_call(
        norm_kernel,
        grid=(tokens // step,),
        in_specs=[pl.BlockSpec((step, model), lambda i: (i, 0))],
        out_specs=(
            pl.BlockSpec((peers, step, own), lambda i: (0, i, 0)),
            pl.BlockSpec((step, LANES), lambda i: (i, 0)),
        ),
        out_shape=(
            jax.ShapeDtypeStruct((peers, tokens, own), jnp.bfloat16),
            jax.ShapeDtypeStruct((tokens, LANES), jnp.float32),
        ),
        compiler_params=LARGE,
    )(layer_input)
    columns = lax.all_to_all(blocks, "fsdp", split_axis=0, concat_axis=0, tiled=True)
    columns = columns.reshape(peers * tokens, own)
    scaled_weight = pl.pallas_call(
        scale_kernel,
        grid=(1,),
        in_specs=[
            pl.BlockSpec((own, width), lambda i: (0, 0)),
            pl.BlockSpec((1, own), lambda i: (0, 0)),
            pl.BlockSpec((16, LANES), lambda i: (0, 0)),
        ],
        out_specs=pl.BlockSpec((width, own), lambda i: (0, 0)),
        out_shape=jax.ShapeDtypeStruct((width, own), jnp.bfloat16),
        compiler_params=LARGE,
        cost_estimate=pl.CostEstimate(
            flops=256 * tokens * model * width, bytes_accessed=4 * own * width, transcendentals=0
        ),
    )(value_weight, norm_gain[None, :], cotangent)
    scaled_weight, columns = lax.optimization_barrier((scaled_weight, columns))
    all_weight = lax.all_gather(scaled_weight, "fsdp", axis=0)

    grad_scale = 1.0 / math.sqrt(cotangent.shape[0])
    grad = lax.dot_general(
        cotangent, columns, (((0,), (0,)), ((), ())), preferred_element_type=jnp.float32
    )
    grad_w = (grad * (norm_gain * grad_scale)[None, :]).astype(jnp.bfloat16)
    weight_t = value_weight.T.astype(jnp.float32)
    grad_g = (jnp.sum(grad * weight_t, axis=0, keepdims=True) * grad_scale).astype(jnp.bfloat16)
    shards = lax.all_to_all(grad_w, "dp", split_axis=0, concat_axis=0, tiled=True)

    sent = kernel_call(
        gram_kernel,
        jax.ShapeDtypeStruct((REPLICAS, 16, LANES), jnp.float32),
        shards,
        grad_g.astype(jnp.float32),
    )
    parts = lax.all_to_all(sent, "dp", split_axis=0, concat_axis=0, tiled=True)
    sent = kernel_call(
        gain_gram_kernel, jax.ShapeDtypeStruct((peers, 16, LANES), jnp.float32), parts
    )
    packed = lax.all_to_all(sent, "fsdp", split_axis=0, concat_axis=0, tiled=True)
    group = 8
    input_grad, done = pl.pallas_call(
        input_kernel,
        grid=(peers // group,),
        in_specs=[
            pl.BlockSpec((tokens, model), lambda i: (0, 0)),
            pl.BlockSpec((tokens, width), lambda i: (0, 0)),
            pl.BlockSpec((group, width, own), lambda i: (i, 0, 0)),
            pl.BlockSpec((tokens, LANES), lambda i: (0, 0)),
        ],
        out_specs=(
            pl.BlockSpec((tokens, model), lambda i: (0, 0)),
            pl.BlockSpec((8, LANES), lambda i: (0, 0)),
        ),
        out_shape=(
            jax.ShapeDtypeStruct((tokens, model), jnp.bfloat16),
            jax.ShapeDtypeStruct((8, LANES), jnp.float32),
        ),
        scratch_shapes=[
            pltpu.VMEM((tokens, model), jnp.bfloat16),
            pltpu.VMEM((tokens, own), jnp.float32),
        ],
        compiler_params=INPUT,
        cost_estimate=pl.CostEstimate(
            flops=2 * tokens * model * width, bytes_accessed=2 * model * (width + 2 * tokens), transcendentals=0
        ),
    )(layer_input, value_cotangent, all_weight, scale)
    weight_update, gain_update = pl.pallas_call(
        combine_kernel,
        out_shape=(
            jax.ShapeDtypeStruct((shards.shape[0] // REPLICAS, own), jnp.bfloat16),
            jax.ShapeDtypeStruct((own,), jnp.bfloat16),
        ),
        compiler_params=PARAMS,
    )(packed, shards, parts, done)
    return (input_grad, weight_update.T, gain_update)


def solution(mesh):
    in_specs = (P(("dp", "fsdp"), None), P("fsdp"), P("fsdp", None), P(("dp", "fsdp"), None))
    out_specs = (P(("dp", "fsdp"), None), P("fsdp", "dp"), P("fsdp"))
    return jax.shard_map(body, mesh=mesh, in_specs=in_specs, out_specs=out_specs, check_vma=False)
```

```python
import math

import jax
import jax.numpy as jnp
from jax import lax
from jax.experimental import pallas as pl
from jax.experimental.pallas import tpu as pltpu
from jax.sharding import PartitionSpec as P

EPS_NORM = 1e-05
EPS_SUM = 1e-06
REPLICAS = 32
LANES = 128
CHUNKS = 4
PARAMS = pltpu.CompilerParams(vmem_limit_bytes=32 * 1024 * 1024)
LARGE = pltpu.CompilerParams(vmem_limit_bytes=60 * 1024 * 1024)


def pack_gram(gram):
    row = lax.broadcasted_iota(jnp.int32, gram.shape, 0)
    lane = lax.broadcasted_iota(jnp.int32, gram.shape, 1)
    kept = jnp.where(row // 8 == lane // REPLICAS, gram, 0.0)
    return kept[0:8] + kept[8:16] + kept[16:24] + kept[24:32]


def unpack_gram(packed):
    tiled = jnp.concatenate([packed] * 4, axis=0)
    row = lax.broadcasted_iota(jnp.int32, tiled.shape, 0)
    lane = lax.broadcasted_iota(jnp.int32, tiled.shape, 1)
    kept = jnp.where(row // 8 == lane // REPLICAS, tiled, 0.0)
    kept = kept + pltpu.roll(kept, 64, 1)
    return kept + pltpu.roll(kept, 32, 1)


def gram_kernel(shards_ref, gain_ref, out_ref):
    shards = shards_ref[...]
    products = lax.dot_general(
        shards, shards, (((1,), (1,)), ((), ())), preferred_element_type=jnp.float32
    )
    rows, width = products.shape[0], shards.shape[0] // REPLICAS
    row = lax.broadcasted_iota(jnp.int32, products.shape, 0)
    column = lax.broadcasted_iota(jnp.int32, products.shape, 1)
    kept = jnp.where(row % width == column % width, products, 0.0)
    folded = jnp.sum(kept.reshape(REPLICAS, width, rows), axis=1)
    source = lax.broadcasted_iota(jnp.int32, (rows, LANES), 0)
    target = lax.broadcasted_iota(jnp.int32, (rows, LANES), 1)
    spread = jnp.where(source // width == target % REPLICAS, 1.0, 0.0)
    gram = jnp.dot(
        folded, spread, precision=lax.Precision.HIGHEST, preferred_element_type=jnp.float32
    )
    packed = pack_gram(gram)
    gain = gain_ref[...]
    for peer in range(out_ref.shape[0]):
        out_ref[peer, 0:8, :] = packed
        for part in range(4):
            out_ref[peer, 8 + part : 9 + part, :] = gain[:, part * LANES : (part + 1) * LANES]
        out_ref[peer, 12:16, :] = jnp.zeros((4, LANES), jnp.float32)


def gain_gram_kernel(parts_ref, out_ref):
    packed = jnp.sum(parts_ref[:, 0:8, :], axis=0)
    gram = jnp.zeros((REPLICAS, REPLICAS), jnp.float32)
    for part in range(4):
        piece = parts_ref[:, 8 + part, :].astype(jnp.bfloat16)
        gram += lax.dot_general(
            piece, piece, (((1,), (1,)), ((), ())), preferred_element_type=jnp.float32
        )
    packed_gain = pack_gram(jnp.concatenate([gram] * 4, axis=1))
    for peer in range(out_ref.shape[0]):
        out_ref[peer, 0:8, :] = packed
        out_ref[peer, 8:16, :] = packed_gain


def swap(values, stride, axis):
    size = values.shape[axis]
    index = lax.broadcasted_iota(jnp.int32, values.shape, axis)
    up = pltpu.roll(values, size - stride, axis)
    down = pltpu.roll(values, stride, axis)
    return jnp.where((index & stride) == 0, up, down)


def pair_weights(gram):
    row = lax.broadcasted_iota(jnp.int32, gram.shape, 0)
    lane = lax.broadcasted_iota(jnp.int32, gram.shape, 1)
    column = lane % REPLICAS
    first = lane < REPLICAS
    weights = jnp.ones((REPLICAS, 1), jnp.float32)
    for stride in (16, 8, 4, 2, 1):
        same = row == column
        met = row == (column ^ stride)

        def coefs(axis, only):
            norm = jnp.sum(jnp.where(same & only, gram, 0.0), axis=axis, keepdims=True)
            inner = jnp.sum(jnp.where(met & only, gram, 0.0), axis=axis, keepdims=True)
            return 1.0 - inner / (2.0 * (jnp.maximum(norm, 0.0) + EPS_SUM))

        down = coefs(1, first)
        weights = weights * down
        if stride > 1:
            scaled = gram * down * coefs(0, True)
            scaled = scaled + swap(scaled, stride, 0)
            gram = scaled + swap(scaled, stride, 1)
    return weights


def combine_kernel(packed_ref, shards_ref, parts_ref, done_ref, weight_ref, gain_ref):
    packed = jnp.sum(packed_ref[...], axis=0)
    weights_w = pair_weights(unpack_gram(packed[0:8]))
    weights_g = pair_weights(unpack_gram(packed[8:16]))
    width = shards_ref.shape[0] // REPLICAS
    total = jnp.zeros((width, shards_ref.shape[1]), jnp.float32)
    for replica in range(REPLICAS):
        shard = shards_ref[replica * width : (replica + 1) * width, :].astype(jnp.float32)
        total += weights_w[replica : replica + 1, :] * shard
    weight_ref[...] = total.astype(jnp.bfloat16)
    gains = [
        jnp.sum(weights_g * parts_ref[:, 8 + part, :], axis=0, keepdims=True) for part in range(4)
    ]
    gain_ref[...] = jnp.concatenate(gains, axis=1)[0].astype(jnp.bfloat16)


def kernel_call(kernel, out_shape, *args):
    return pl.pallas_call(
        kernel,
        out_shape=out_shape,
        compiler_params=PARAMS,
    )(*args)


def norm_kernel(input_ref, blocks_ref, scale_ref):
    input32 = input_ref[...].astype(jnp.float32)
    square = jnp.mean(input32 * input32, axis=1, keepdims=True)
    inverse_rms = lax.rsqrt(square + EPS_NORM)
    scale_ref[...] = jnp.broadcast_to(inverse_rms, scale_ref.shape)
    normed = (input32 * inverse_rms).astype(jnp.bfloat16)
    width = blocks_ref.shape[2]
    for owner in range(blocks_ref.shape[0]):
        blocks_ref[owner, :, :] = normed[:, owner * width : (owner + 1) * width]


def input_kernel(
    input_hbm,
    cotangent_hbm,
    weight_hbm,
    scale_hbm,
    out_hbm,
    done_hbm,
    input_ref,
    cotangent_ref,
    weight_ref,
    scale_ref,
    hat_ref,
    out_ref,
    input_sem,
    small_sem,
    weight_sem,
    out_sem,
):
    blocks, width = weight_ref.shape[0], weight_ref.shape[2]
    chunk = blocks // CHUNKS
    small = [
        pltpu.make_async_copy(cotangent_hbm, cotangent_ref, small_sem.at[0]),
        pltpu.make_async_copy(scale_hbm, scale_ref, small_sem.at[1]),
    ]
    small[0].start()
    arriving = []
    for part in range(CHUNKS):
        at = pl.ds(part * chunk, chunk)
        columns = pl.ds(part * chunk * width, chunk * width)
        pair = [
            pltpu.make_async_copy(weight_hbm.at[at], weight_ref.at[at], weight_sem.at[part]),
            pltpu.make_async_copy(
                input_hbm.at[:, columns], input_ref.at[:, columns], input_sem.at[part]
            ),
        ]
        for copy in pair:
            copy.start()
        arriving.append(pair)
    small[1].start()
    small[0].wait()
    cotangent = cotangent_ref[...]
    total = jnp.zeros((cotangent.shape[0], LANES), jnp.float32)
    for block in range(blocks):
        if block % chunk == 0:
            for copy in arriving[block // chunk]:
                copy.wait()
        columns = slice(block * width, (block + 1) * width)
        hat = jnp.dot(cotangent, weight_ref[block], preferred_element_type=jnp.float32).astype(
            jnp.bfloat16
        )
        hat_ref[:, columns] = hat
        terms = hat.astype(jnp.float32) * input_ref[:, columns].astype(jnp.float32)
        for lane in range(0, width, LANES):
            total += terms[:, lane : lane + LANES]
    small[1].wait()
    inverse_rms = scale_ref[:, 0:1]
    factor = jnp.sum(total, axis=1, keepdims=True) / (blocks * width)
    factor = inverse_rms * inverse_rms * factor
    leaving = []
    for part in range(CHUNKS):
        for block in range(part * chunk, (part + 1) * chunk):
            columns = slice(block * width, (block + 1) * width)
            piece = input_ref[:, columns].astype(jnp.float32)
            out_ref[:, columns] = (
                inverse_rms * (hat_ref[:, columns].astype(jnp.float32) - piece * factor)
            ).astype(jnp.bfloat16)
        at = pl.ds(part * chunk * width, chunk * width)
        copy = pltpu.make_async_copy(out_ref.at[:, at], out_hbm.at[:, at], out_sem.at[part])
        copy.start()
        leaving.append(copy)
    for copy in leaving:
        copy.wait()


def gate_kernel(value_ref, after_ref, out_ref):
    pass


def body(layer_input, norm_gain, value_weight, value_cotangent):
    tokens, model = layer_input.shape
    peers, width = lax.axis_size("fsdp"), value_cotangent.shape[1]
    own = model // peers
    cotangent = lax.all_gather(value_cotangent, "fsdp", axis=0, tiled=True)
    step = 64
    blocks, scale = pl.pallas_call(
        norm_kernel,
        grid=(tokens // step,),
        in_specs=[pl.BlockSpec((step, model), lambda i: (i, 0))],
        out_specs=(
            pl.BlockSpec((peers, step, own), lambda i: (0, i, 0)),
            pl.BlockSpec((step, LANES), lambda i: (i, 0)),
        ),
        out_shape=(
            jax.ShapeDtypeStruct((peers, tokens, own), jnp.bfloat16),
            jax.ShapeDtypeStruct((tokens, LANES), jnp.float32),
        ),
        compiler_params=LARGE,
    )(layer_input)
    columns = lax.all_to_all(blocks, "fsdp", split_axis=0, concat_axis=0, tiled=True)
    columns = columns.reshape(peers * tokens, own)
    weight_t = value_weight.T.astype(jnp.float32)
    scaled_weight = (weight_t * norm_gain[None, :]).astype(jnp.bfloat16)
    hbm = pl.BlockSpec(memory_space=pltpu.HBM)
    scaled_weight = pl.pallas_call(
        gate_kernel,
        in_specs=[hbm, hbm],
        out_specs=hbm,
        out_shape=jax.ShapeDtypeStruct((width, own), jnp.bfloat16),
        input_output_aliases={0: 0},
        compiler_params=LARGE,
        cost_estimate=pl.CostEstimate(
            flops=256 * tokens * model * width, bytes_accessed=4 * own * width, transcendentals=0
        ),
    )(scaled_weight, cotangent)
    scaled_weight, columns = lax.optimization_barrier((scaled_weight, columns))
    all_weight = lax.all_gather(scaled_weight, "fsdp", axis=0)

    grad_scale = 1.0 / math.sqrt(cotangent.shape[0])
    grad = lax.dot_general(
        cotangent, columns, (((0,), (0,)), ((), ())), preferred_element_type=jnp.float32
    )
    grad_w = (grad * (norm_gain * grad_scale)[None, :]).astype(jnp.bfloat16)
    grad_g = (jnp.sum(grad * weight_t, axis=0, keepdims=True) * grad_scale).astype(jnp.bfloat16)
    shards = lax.all_to_all(grad_w, "dp", split_axis=0, concat_axis=0, tiled=True)

    sent = kernel_call(
        gram_kernel,
        jax.ShapeDtypeStruct((REPLICAS, 16, LANES), jnp.float32),
        shards,
        grad_g.astype(jnp.float32),
    )
    parts = lax.all_to_all(sent, "dp", split_axis=0, concat_axis=0, tiled=True)
    sent = kernel_call(
        gain_gram_kernel, jax.ShapeDtypeStruct((peers, 16, LANES), jnp.float32), parts
    )
    packed = lax.all_to_all(sent, "fsdp", split_axis=0, concat_axis=0, tiled=True)
    vmem = pl.BlockSpec(memory_space=pltpu.VMEM)
    input_grad, done = pl.pallas_call(
        input_kernel,
        in_specs=[hbm, hbm, hbm, hbm],
        out_specs=(hbm, hbm),
        out_shape=(
            jax.ShapeDtypeStruct((tokens, model), jnp.bfloat16),
            jax.ShapeDtypeStruct((8, LANES), jnp.float32),
        ),
        scratch_shapes=[
            pltpu.VMEM((tokens, model), jnp.bfloat16),
            pltpu.VMEM((tokens, width), jnp.bfloat16),
            pltpu.VMEM((peers, width, own), jnp.bfloat16),
            pltpu.VMEM((tokens, LANES), jnp.float32),
            pltpu.VMEM((tokens, model), jnp.bfloat16),
            pltpu.VMEM((tokens, model), jnp.bfloat16),
            pltpu.SemaphoreType.DMA((CHUNKS,)),
            pltpu.SemaphoreType.DMA((2,)),
            pltpu.SemaphoreType.DMA((CHUNKS,)),
            pltpu.SemaphoreType.DMA((CHUNKS,)),
        ],
        compiler_params=LARGE,
        cost_estimate=pl.CostEstimate(
            flops=2 * tokens * model * width, bytes_accessed=2 * model * (width + 2 * tokens), transcendentals=0
        ),
    )(layer_input, value_cotangent, all_weight, scale)
    weight_update, gain_update = pl.pallas_call(
        combine_kernel,
        in_specs=[vmem, vmem, vmem, hbm],
        out_shape=(
            jax.ShapeDtypeStruct((shards.shape[0] // REPLICAS, own), jnp.bfloat16),
            jax.ShapeDtypeStruct((own,), jnp.bfloat16),
        ),
        compiler_params=PARAMS,
    )(packed, shards, parts, done)
    return (input_grad, weight_update.T, gain_update)


def solution(mesh):
    in_specs = (P(("dp", "fsdp"), None), P("fsdp"), P("fsdp", None), P(("dp", "fsdp"), None))
    out_specs = (P(("dp", "fsdp"), None), P("fsdp", "dp"), P("fsdp"))
    return jax.shard_map(body, mesh=mesh, in_specs=in_specs, out_specs=out_specs, check_vma=False)
```

```python
import math

import jax
import jax.numpy as jnp
from jax import lax
from jax.experimental import pallas as pl
from jax.experimental.pallas import tpu as pltpu
from jax.sharding import PartitionSpec as P

EPS_NORM = 1e-05
EPS_SUM = 1e-06
REPLICAS = 32
LANES = 128
CHUNKS = 4
PARAMS = pltpu.CompilerParams(vmem_limit_bytes=32 * 1024 * 1024)
LARGE = pltpu.CompilerParams(vmem_limit_bytes=60 * 1024 * 1024)


def pack_gram(gram):
    row = lax.broadcasted_iota(jnp.int32, gram.shape, 0)
    lane = lax.broadcasted_iota(jnp.int32, gram.shape, 1)
    kept = jnp.where(row // 8 == lane // REPLICAS, gram, 0.0)
    return kept[0:8] + kept[8:16] + kept[16:24] + kept[24:32]


def unpack_gram(packed):
    tiled = jnp.concatenate([packed] * 4, axis=0)
    row = lax.broadcasted_iota(jnp.int32, tiled.shape, 0)
    lane = lax.broadcasted_iota(jnp.int32, tiled.shape, 1)
    kept = jnp.where(row // 8 == lane // REPLICAS, tiled, 0.0)
    kept = kept + pltpu.roll(kept, 64, 1)
    return kept + pltpu.roll(kept, 32, 1)


def gram_kernel(shards_ref, gain_ref, out_ref):
    shards = shards_ref[...]
    products = lax.dot_general(
        shards, shards, (((1,), (1,)), ((), ())), preferred_element_type=jnp.float32
    )
    rows, width = products.shape[0], shards.shape[0] // REPLICAS
    row = lax.broadcasted_iota(jnp.int32, products.shape, 0)
    column = lax.broadcasted_iota(jnp.int32, products.shape, 1)
    kept = jnp.where(row % width == column % width, products, 0.0)
    folded = jnp.sum(kept.reshape(REPLICAS, width, rows), axis=1)
    source = lax.broadcasted_iota(jnp.int32, (rows, LANES), 0)
    target = lax.broadcasted_iota(jnp.int32, (rows, LANES), 1)
    spread = jnp.where(source // width == target % REPLICAS, 1.0, 0.0)
    gram = jnp.dot(
        folded, spread, precision=lax.Precision.HIGHEST, preferred_element_type=jnp.float32
    )
    packed = pack_gram(gram)
    gain = gain_ref[...]
    for peer in range(out_ref.shape[0]):
        out_ref[peer, 0:8, :] = packed
        for part in range(4):
            out_ref[peer, 8 + part : 9 + part, :] = gain[:, part * LANES : (part + 1) * LANES]
        out_ref[peer, 12:16, :] = jnp.zeros((4, LANES), jnp.float32)


def gain_gram_kernel(parts_ref, out_ref):
    packed = jnp.sum(parts_ref[:, 0:8, :], axis=0)
    gram = jnp.zeros((REPLICAS, REPLICAS), jnp.float32)
    for part in range(4):
        piece = parts_ref[:, 8 + part, :].astype(jnp.bfloat16)
        gram += lax.dot_general(
            piece, piece, (((1,), (1,)), ((), ())), preferred_element_type=jnp.float32
        )
    packed_gain = pack_gram(jnp.concatenate([gram] * 4, axis=1))
    for peer in range(out_ref.shape[0]):
        out_ref[peer, 0:8, :] = packed
        out_ref[peer, 8:16, :] = packed_gain


def swap(values, stride, axis):
    size = values.shape[axis]
    index = lax.broadcasted_iota(jnp.int32, values.shape, axis)
    up = pltpu.roll(values, size - stride, axis)
    down = pltpu.roll(values, stride, axis)
    return jnp.where((index & stride) == 0, up, down)


def pair_weights(gram):
    row = lax.broadcasted_iota(jnp.int32, gram.shape, 0)
    lane = lax.broadcasted_iota(jnp.int32, gram.shape, 1)
    column = lane % REPLICAS
    first = lane < REPLICAS
    weights = jnp.ones((REPLICAS, 1), jnp.float32)
    for stride in (16, 8, 4, 2, 1):
        same = row == column
        met = row == (column ^ stride)

        def coefs(axis, only):
            norm = jnp.sum(jnp.where(same & only, gram, 0.0), axis=axis, keepdims=True)
            inner = jnp.sum(jnp.where(met & only, gram, 0.0), axis=axis, keepdims=True)
            return 1.0 - inner / (2.0 * (jnp.maximum(norm, 0.0) + EPS_SUM))

        down = coefs(1, first)
        weights = weights * down
        if stride > 1:
            scaled = gram * down * coefs(0, True)
            scaled = scaled + swap(scaled, stride, 0)
            gram = scaled + swap(scaled, stride, 1)
    return weights


def combine_kernel(packed_ref, shards_ref, parts_ref, weight_ref, gain_ref):
    packed = jnp.sum(packed_ref[...], axis=0)
    weights_w = pair_weights(unpack_gram(packed[0:8]))
    weights_g = pair_weights(unpack_gram(packed[8:16]))
    width = shards_ref.shape[0] // REPLICAS
    total = jnp.zeros((width, shards_ref.shape[1]), jnp.float32)
    for replica in range(REPLICAS):
        shard = shards_ref[replica * width : (replica + 1) * width, :].astype(jnp.float32)
        total += weights_w[replica : replica + 1, :] * shard
    weight_ref[...] = total.astype(jnp.bfloat16)
    gains = [
        jnp.sum(weights_g * parts_ref[:, 8 + part, :], axis=0, keepdims=True) for part in range(4)
    ]
    gain_ref[...] = jnp.concatenate(gains, axis=1)[0].astype(jnp.bfloat16)


def kernel_call(kernel, out_shape, *args):
    return pl.pallas_call(
        kernel,
        out_shape=out_shape,
        compiler_params=PARAMS,
    )(*args)


def norm_kernel(input_ref, blocks_ref, scale_ref):
    input32 = input_ref[...].astype(jnp.float32)
    square = jnp.mean(input32 * input32, axis=1, keepdims=True)
    inverse_rms = lax.rsqrt(square + EPS_NORM)
    scale_ref[...] = jnp.broadcast_to(inverse_rms, scale_ref.shape)
    normed = (input32 * inverse_rms).astype(jnp.bfloat16)
    width = blocks_ref.shape[2]
    for owner in range(blocks_ref.shape[0]):
        blocks_ref[owner, :, :] = normed[:, owner * width : (owner + 1) * width]


def input_kernel(
    input_hbm,
    cotangent_hbm,
    weight_hbm,
    scale_hbm,
    out_hbm,
    input_ref,
    cotangent_ref,
    weight_ref,
    scale_ref,
    hat_ref,
    out_ref,
    input_sem,
    small_sem,
    weight_sem,
    out_sem,
):
    blocks, width = weight_ref.shape[0], weight_ref.shape[2]
    chunk = blocks // CHUNKS
    small = [
        pltpu.make_async_copy(cotangent_hbm, cotangent_ref, small_sem.at[0]),
        pltpu.make_async_copy(scale_hbm, scale_ref, small_sem.at[1]),
    ]
    small[0].start()
    arriving = []
    for part in range(CHUNKS):
        at = pl.ds(part * chunk, chunk)
        columns = pl.ds(part * chunk * width, chunk * width)
        pair = [
            pltpu.make_async_copy(weight_hbm.at[at], weight_ref.at[at], weight_sem.at[part]),
            pltpu.make_async_copy(
                input_hbm.at[:, columns], input_ref.at[:, columns], input_sem.at[part]
            ),
        ]
        for copy in pair:
            copy.start()
        arriving.append(pair)
    small[1].start()
    small[0].wait()
    cotangent = cotangent_ref[...]
    total = jnp.zeros((cotangent.shape[0], LANES), jnp.float32)
    for block in range(blocks):
        if block % chunk == 0:
            for copy in arriving[block // chunk]:
                copy.wait()
        columns = slice(block * width, (block + 1) * width)
        hat = jnp.dot(cotangent, weight_ref[block], preferred_element_type=jnp.float32).astype(
            jnp.bfloat16
        )
        hat_ref[:, columns] = hat
        terms = hat.astype(jnp.float32) * input_ref[:, columns].astype(jnp.float32)
        for lane in range(0, width, LANES):
            total += terms[:, lane : lane + LANES]
    small[1].wait()
    inverse_rms = scale_ref[:, 0:1]
    factor = jnp.sum(total, axis=1, keepdims=True) / (blocks * width)
    factor = inverse_rms * inverse_rms * factor
    leaving = []
    for part in range(CHUNKS):
        for block in range(part * chunk, (part + 1) * chunk):
            columns = slice(block * width, (block + 1) * width)
            piece = input_ref[:, columns].astype(jnp.float32)
            out_ref[:, columns] = (
                inverse_rms * (hat_ref[:, columns].astype(jnp.float32) - piece * factor)
            ).astype(jnp.bfloat16)
        at = pl.ds(part * chunk * width, chunk * width)
        copy = pltpu.make_async_copy(out_ref.at[:, at], out_hbm.at[:, at], out_sem.at[part])
        copy.start()
        leaving.append(copy)
    for copy in leaving:
        copy.wait()


def gate_kernel(value_ref, after_ref, out_ref):
    pass


def body(layer_input, norm_gain, value_weight, value_cotangent):
    tokens, model = layer_input.shape
    peers, width = lax.axis_size("fsdp"), value_cotangent.shape[1]
    own = model // peers
    cotangent = lax.all_gather(value_cotangent, "fsdp", axis=0, tiled=True)
    step = 64
    blocks, scale = pl.pallas_call(
        norm_kernel,
        grid=(tokens // step,),
        in_specs=[pl.BlockSpec((step, model), lambda i: (i, 0))],
        out_specs=(
            pl.BlockSpec((peers, step, own), lambda i: (0, i, 0)),
            pl.BlockSpec((step, LANES), lambda i: (i, 0)),
        ),
        out_shape=(
            jax.ShapeDtypeStruct((peers, tokens, own), jnp.bfloat16),
            jax.ShapeDtypeStruct((tokens, LANES), jnp.float32),
        ),
        compiler_params=LARGE,
    )(layer_input)
    columns = lax.all_to_all(blocks, "fsdp", split_axis=0, concat_axis=0, tiled=True)
    columns = columns.reshape(peers * tokens, own)
    weight_t = value_weight.T.astype(jnp.float32)
    scaled_weight = (weight_t * norm_gain[None, :]).astype(jnp.bfloat16)
    hbm = pl.BlockSpec(memory_space=pltpu.HBM)
    scaled_weight = pl.pallas_call(
        gate_kernel,
        in_specs=[hbm, hbm],
        out_specs=hbm,
        out_shape=jax.ShapeDtypeStruct((width, own), jnp.bfloat16),
        input_output_aliases={0: 0},
        compiler_params=LARGE,
        cost_estimate=pl.CostEstimate(
            flops=256 * tokens * model * width, bytes_accessed=4 * own * width, transcendentals=0
        ),
    )(scaled_weight, cotangent)
    scaled_weight, columns = lax.optimization_barrier((scaled_weight, columns))
    all_weight = lax.all_gather(scaled_weight, "fsdp", axis=0)

    grad_scale = 1.0 / math.sqrt(cotangent.shape[0])
    grad = lax.dot_general(
        cotangent, columns, (((0,), (0,)), ((), ())), preferred_element_type=jnp.float32
    )
    grad_w = (grad * (norm_gain * grad_scale)[None, :]).astype(jnp.bfloat16)
    grad_g = (jnp.sum(grad * weight_t, axis=0, keepdims=True) * grad_scale).astype(jnp.bfloat16)
    shards = lax.all_to_all(grad_w, "dp", split_axis=0, concat_axis=0, tiled=True)

    sent = kernel_call(
        gram_kernel,
        jax.ShapeDtypeStruct((REPLICAS, 16, LANES), jnp.float32),
        shards,
        grad_g.astype(jnp.float32),
    )
    parts = lax.all_to_all(sent, "dp", split_axis=0, concat_axis=0, tiled=True)
    sent = kernel_call(
        gain_gram_kernel, jax.ShapeDtypeStruct((peers, 16, LANES), jnp.float32), parts
    )
    packed = lax.all_to_all(sent, "fsdp", split_axis=0, concat_axis=0, tiled=True)
    input_grad = pl.pallas_call(
        input_kernel,
        in_specs=[hbm, hbm, hbm, hbm],
        out_specs=hbm,
        out_shape=jax.ShapeDtypeStruct((tokens, model), jnp.bfloat16),
        scratch_shapes=[
            pltpu.VMEM((tokens, model), jnp.bfloat16),
            pltpu.VMEM((tokens, width), jnp.bfloat16),
            pltpu.VMEM((peers, width, own), jnp.bfloat16),
            pltpu.VMEM((tokens, LANES), jnp.float32),
            pltpu.VMEM((tokens, model), jnp.bfloat16),
            pltpu.VMEM((tokens, model), jnp.bfloat16),
            pltpu.SemaphoreType.DMA((CHUNKS,)),
            pltpu.SemaphoreType.DMA((2,)),
            pltpu.SemaphoreType.DMA((CHUNKS,)),
            pltpu.SemaphoreType.DMA((CHUNKS,)),
        ],
        compiler_params=LARGE,
        cost_estimate=pl.CostEstimate(
            flops=2 * tokens * model * width, bytes_accessed=2 * model * (width + 2 * tokens), transcendentals=0
        ),
    )(layer_input, value_cotangent, all_weight, scale)
    weight_update, gain_update = pl.pallas_call(
        combine_kernel,
        out_shape=(
            jax.ShapeDtypeStruct((shards.shape[0] // REPLICAS, own), jnp.bfloat16),
            jax.ShapeDtypeStruct((own,), jnp.bfloat16),
        ),
        compiler_params=PARAMS,
    )(packed, shards, parts)
    return (input_grad, weight_update.T, gain_update)


def solution(mesh):
    in_specs = (P(("dp", "fsdp"), None), P("fsdp"), P("fsdp", None), P(("dp", "fsdp"), None))
    out_specs = (P(("dp", "fsdp"), None), P("fsdp", "dp"), P("fsdp"))
    return jax.shard_map(body, mesh=mesh, in_specs=in_specs, out_specs=out_specs, check_vma=False)
```

```python
import math

import jax
import jax.numpy as jnp
from jax import lax
from jax.experimental import pallas as pl
from jax.experimental.pallas import tpu as pltpu
from jax.sharding import PartitionSpec as P

EPS_NORM = 1e-05
EPS_SUM = 1e-06
REPLICAS = 32
LANES = 128
CHUNKS = 4
PARAMS = pltpu.CompilerParams(vmem_limit_bytes=32 * 1024 * 1024)
INPUT = pltpu.CompilerParams(vmem_limit_bytes=46 * 1024 * 1024)
LARGE = pltpu.CompilerParams(vmem_limit_bytes=60 * 1024 * 1024)


def pack_gram(gram):
    row = lax.broadcasted_iota(jnp.int32, gram.shape, 0)
    lane = lax.broadcasted_iota(jnp.int32, gram.shape, 1)
    kept = jnp.where(row // 8 == lane // REPLICAS, gram, 0.0)
    return kept[0:8] + kept[8:16] + kept[16:24] + kept[24:32]


def unpack_gram(packed):
    tiled = jnp.concatenate([packed] * 4, axis=0)
    row = lax.broadcasted_iota(jnp.int32, tiled.shape, 0)
    lane = lax.broadcasted_iota(jnp.int32, tiled.shape, 1)
    kept = jnp.where(row // 8 == lane // REPLICAS, tiled, 0.0)
    kept = kept + pltpu.roll(kept, 64, 1)
    return kept + pltpu.roll(kept, 32, 1)


def gram_kernel(shards_ref, gain_ref, out_ref):
    shards = shards_ref[...]
    products = lax.dot_general(
        shards, shards, (((1,), (1,)), ((), ())), preferred_element_type=jnp.float32
    )
    rows, width = products.shape[0], shards.shape[0] // REPLICAS
    row = lax.broadcasted_iota(jnp.int32, products.shape, 0)
    column = lax.broadcasted_iota(jnp.int32, products.shape, 1)
    kept = jnp.where(row % width == column % width, products, 0.0)
    folded = jnp.sum(kept.reshape(REPLICAS, width, rows), axis=1)
    source = lax.broadcasted_iota(jnp.int32, (rows, LANES), 0)
    target = lax.broadcasted_iota(jnp.int32, (rows, LANES), 1)
    spread = jnp.where(source // width == target % REPLICAS, 1.0, 0.0)
    gram = jnp.dot(
        folded, spread, precision=lax.Precision.HIGHEST, preferred_element_type=jnp.float32
    )
    packed = pack_gram(gram)
    gain = gain_ref[...]
    for peer in range(out_ref.shape[0]):
        out_ref[peer, 0:8, :] = packed
        for part in range(4):
            out_ref[peer, 8 + part : 9 + part, :] = gain[:, part * LANES : (part + 1) * LANES]
        out_ref[peer, 12:16, :] = jnp.zeros((4, LANES), jnp.float32)


def gain_gram_kernel(parts_ref, out_ref):
    packed = jnp.sum(parts_ref[:, 0:8, :], axis=0)
    gram = jnp.zeros((REPLICAS, REPLICAS), jnp.float32)
    for part in range(4):
        piece = parts_ref[:, 8 + part, :].astype(jnp.bfloat16)
        gram += lax.dot_general(
            piece, piece, (((1,), (1,)), ((), ())), preferred_element_type=jnp.float32
        )
    packed_gain = pack_gram(jnp.concatenate([gram] * 4, axis=1))
    for peer in range(out_ref.shape[0]):
        out_ref[peer, 0:8, :] = packed
        out_ref[peer, 8:16, :] = packed_gain


def swap(values, stride, axis):
    size = values.shape[axis]
    index = lax.broadcasted_iota(jnp.int32, values.shape, axis)
    up = pltpu.roll(values, size - stride, axis)
    down = pltpu.roll(values, stride, axis)
    return jnp.where((index & stride) == 0, up, down)


def pair_weights(gram):
    row = lax.broadcasted_iota(jnp.int32, gram.shape, 0)
    lane = lax.broadcasted_iota(jnp.int32, gram.shape, 1)
    column = lane % REPLICAS
    first = lane < REPLICAS
    weights = jnp.ones((REPLICAS, 1), jnp.float32)
    for stride in (16, 8, 4, 2, 1):
        same = row == column
        met = row == (column ^ stride)

        def coefs(axis, only):
            norm = jnp.sum(jnp.where(same & only, gram, 0.0), axis=axis, keepdims=True)
            inner = jnp.sum(jnp.where(met & only, gram, 0.0), axis=axis, keepdims=True)
            return 1.0 - inner / (2.0 * (jnp.maximum(norm, 0.0) + EPS_SUM))

        down = coefs(1, first)
        weights = weights * down
        if stride > 1:
            scaled = gram * down * coefs(0, True)
            scaled = scaled + swap(scaled, stride, 0)
            gram = scaled + swap(scaled, stride, 1)
    return weights


def combine_kernel(packed_ref, shards_ref, parts_ref, weight_ref, gain_ref):
    packed = jnp.sum(packed_ref[...], axis=0)
    weights_w = pair_weights(unpack_gram(packed[0:8]))
    weights_g = pair_weights(unpack_gram(packed[8:16]))
    width = shards_ref.shape[0] // REPLICAS
    total = jnp.zeros((width, shards_ref.shape[1]), jnp.float32)
    for replica in range(REPLICAS):
        shard = shards_ref[replica * width : (replica + 1) * width, :].astype(jnp.float32)
        total += weights_w[replica : replica + 1, :] * shard
    weight_ref[...] = total.astype(jnp.bfloat16)
    gains = [
        jnp.sum(weights_g * parts_ref[:, 8 + part, :], axis=0, keepdims=True) for part in range(4)
    ]
    gain_ref[...] = jnp.concatenate(gains, axis=1)[0].astype(jnp.bfloat16)


def kernel_call(kernel, out_shape, *args):
    return pl.pallas_call(
        kernel,
        out_shape=out_shape,
        compiler_params=PARAMS,
    )(*args)


def norm_kernel(input_ref, blocks_ref, scale_ref):
    input32 = input_ref[...].astype(jnp.float32)
    square = jnp.mean(input32 * input32, axis=1, keepdims=True)
    inverse_rms = lax.rsqrt(square + EPS_NORM)
    scale_ref[...] = jnp.broadcast_to(inverse_rms, scale_ref.shape)
    normed = (input32 * inverse_rms).astype(jnp.bfloat16)
    width = blocks_ref.shape[2]
    for owner in range(blocks_ref.shape[0]):
        blocks_ref[owner, :, :] = normed[:, owner * width : (owner + 1) * width]


def input_kernel(
    input_ref,
    cotangent_hbm,
    weight_hbm,
    scale_hbm,
    out_hbm,
    cotangent_ref,
    weight_ref,
    scale_ref,
    hat_ref,
    out_ref,
    small_sem,
    weight_sem,
    out_sem,
):
    blocks, width = weight_ref.shape[0], weight_ref.shape[2]
    chunk = blocks // CHUNKS
    small = [
        pltpu.make_async_copy(cotangent_hbm, cotangent_ref, small_sem.at[0]),
        pltpu.make_async_copy(scale_hbm, scale_ref, small_sem.at[1]),
    ]
    small[0].start()
    arriving = []
    for part in range(CHUNKS):
        at = pl.ds(part * chunk, chunk)
        copy = pltpu.make_async_copy(weight_hbm.at[at], weight_ref.at[at], weight_sem.at[part])
        copy.start()
        arriving.append(copy)
    small[1].start()
    small[0].wait()
    cotangent = cotangent_ref[...]
    total = jnp.zeros((cotangent.shape[0], LANES), jnp.float32)
    for block in range(blocks):
        if block % chunk == 0:
            arriving[block // chunk].wait()
        columns = slice(block * width, (block + 1) * width)
        hat = jnp.dot(cotangent, weight_ref[block], preferred_element_type=jnp.float32).astype(
            jnp.bfloat16
        )
        hat_ref[:, columns] = hat
        terms = hat.astype(jnp.float32) * input_ref[:, columns].astype(jnp.float32)
        for lane in range(0, width, LANES):
            total += terms[:, lane : lane + LANES]
    small[1].wait()
    inverse_rms = scale_ref[:, 0:1]
    factor = jnp.sum(total, axis=1, keepdims=True) / (blocks * width)
    factor = inverse_rms * inverse_rms * factor
    leaving = []
    for part in range(CHUNKS):
        for block in range(part * chunk, (part + 1) * chunk):
            columns = slice(block * width, (block + 1) * width)
            piece = input_ref[:, columns].astype(jnp.float32)
            out_ref[:, columns] = (
                inverse_rms * (hat_ref[:, columns].astype(jnp.float32) - piece * factor)
            ).astype(jnp.bfloat16)
        at = pl.ds(part * chunk * width, chunk * width)
        copy = pltpu.make_async_copy(out_ref.at[:, at], out_hbm.at[:, at], out_sem.at[part])
        copy.start()
        leaving.append(copy)
    for copy in leaving:
        copy.wait()


def gate_kernel(value_ref, after_ref, out_ref):
    pass


def body(layer_input, norm_gain, value_weight, value_cotangent):
    tokens, model = layer_input.shape
    peers, width = lax.axis_size("fsdp"), value_cotangent.shape[1]
    own = model // peers
    cotangent = lax.all_gather(value_cotangent, "fsdp", axis=0, tiled=True)
    step = 64
    blocks, scale = pl.pallas_call(
        norm_kernel,
        grid=(tokens // step,),
        in_specs=[pl.BlockSpec((step, model), lambda i: (i, 0))],
        out_specs=(
            pl.BlockSpec((peers, step, own), lambda i: (0, i, 0)),
            pl.BlockSpec((step, LANES), lambda i: (i, 0)),
        ),
        out_shape=(
            jax.ShapeDtypeStruct((peers, tokens, own), jnp.bfloat16),
            jax.ShapeDtypeStruct((tokens, LANES), jnp.float32),
        ),
        compiler_params=LARGE,
    )(layer_input)
    columns = lax.all_to_all(blocks, "fsdp", split_axis=0, concat_axis=0, tiled=True)
    columns = columns.reshape(peers * tokens, own)
    weight_t = value_weight.T.astype(jnp.float32)
    scaled_weight = (weight_t * norm_gain[None, :]).astype(jnp.bfloat16)
    hbm = pl.BlockSpec(memory_space=pltpu.HBM)
    scaled_weight = pl.pallas_call(
        gate_kernel,
        in_specs=[hbm, hbm],
        out_specs=hbm,
        out_shape=jax.ShapeDtypeStruct((width, own), jnp.bfloat16),
        input_output_aliases={0: 0},
        compiler_params=LARGE,
        cost_estimate=pl.CostEstimate(
            flops=256 * tokens * model * width, bytes_accessed=4 * own * width, transcendentals=0
        ),
    )(scaled_weight, cotangent)
    scaled_weight, columns = lax.optimization_barrier((scaled_weight, columns))
    all_weight = lax.all_gather(scaled_weight, "fsdp", axis=0)

    grad_scale = 1.0 / math.sqrt(cotangent.shape[0])
    grad = lax.dot_general(
        cotangent, columns, (((0,), (0,)), ((), ())), preferred_element_type=jnp.float32
    )
    grad_w = (grad * (norm_gain * grad_scale)[None, :]).astype(jnp.bfloat16)
    grad_g = (jnp.sum(grad * weight_t, axis=0, keepdims=True) * grad_scale).astype(jnp.bfloat16)
    shards = lax.all_to_all(grad_w, "dp", split_axis=0, concat_axis=0, tiled=True)

    sent = kernel_call(
        gram_kernel,
        jax.ShapeDtypeStruct((REPLICAS, 16, LANES), jnp.float32),
        shards,
        grad_g.astype(jnp.float32),
    )
    parts = lax.all_to_all(sent, "dp", split_axis=0, concat_axis=0, tiled=True)
    sent = kernel_call(
        gain_gram_kernel, jax.ShapeDtypeStruct((peers, 16, LANES), jnp.float32), parts
    )
    packed = lax.all_to_all(sent, "fsdp", split_axis=0, concat_axis=0, tiled=True)
    input_grad = pl.pallas_call(
        input_kernel,
        in_specs=[pl.BlockSpec(memory_space=pltpu.VMEM), hbm, hbm, hbm],
        out_specs=hbm,
        out_shape=jax.ShapeDtypeStruct((tokens, model), jnp.bfloat16),
        scratch_shapes=[
            pltpu.VMEM((tokens, width), jnp.bfloat16),
            pltpu.VMEM((peers, width, own), jnp.bfloat16),
            pltpu.VMEM((tokens, LANES), jnp.float32),
            pltpu.VMEM((tokens, model), jnp.bfloat16),
            pltpu.VMEM((tokens, model), jnp.bfloat16),
            pltpu.SemaphoreType.DMA((2,)),
            pltpu.SemaphoreType.DMA((CHUNKS,)),
            pltpu.SemaphoreType.DMA((CHUNKS,)),
        ],
        compiler_params=INPUT,
        cost_estimate=pl.CostEstimate(
            flops=2 * tokens * model * width, bytes_accessed=2 * model * (width + 2 * tokens), transcendentals=0
        ),
    )(layer_input, value_cotangent, all_weight, scale)
    weight_update, gain_update = pl.pallas_call(
        combine_kernel,
        out_shape=(
            jax.ShapeDtypeStruct((shards.shape[0] // REPLICAS, own), jnp.bfloat16),
            jax.ShapeDtypeStruct((own,), jnp.bfloat16),
        ),
        compiler_params=PARAMS,
    )(packed, shards, parts)
    return (input_grad, weight_update.T, gain_update)


def solution(mesh):
    in_specs = (P(("dp", "fsdp"), None), P("fsdp"), P("fsdp", None), P(("dp", "fsdp"), None))
    out_specs = (P(("dp", "fsdp"), None), P("fsdp", "dp"), P("fsdp"))
    return jax.shard_map(body, mesh=mesh, in_specs=in_specs, out_specs=out_specs, check_vma=False)
```
